32 devices in a mesh: grp: 2 (over y), gx: 4 (over z), gy: 4 (over x, core).
Axes of the slice: x: 2, y: 2, z: 4, core: 2. Of those that a mesh axis runs over, the one named last changes fastest.
Arguments:
- tokens: bfloat16 [1024, 8192], P(('grp', 'gy'), 'gx'), parts along dimension 0, may hold values from -6 to 6
- gate_weight: bfloat16 [8192, 26624], P(None, ('gy', 'gx')), may hold values from -0.0625 to 0.0625
- up_weight: bfloat16 [8192, 26624], P(None, ('gy', 'gx')), may hold values from -0.0625 to 0.0625
- down_weight: bfloat16 [26624, 8192], P('gy', 'gx'), may hold values from -0.0390625 to 0.0390625
Outputs:
- mixed: bfloat16 [1024, 8192], P(('grp', 'gy'), 'gx'), parts along dimension 0
The draws below stay inside these ranges and needn't reach their ends.
There are 2 independent parts, one for each index of `grp`. The reference program is written for one: setup_inputs(seed, part) draws one part's arguments, and reference() takes and returns one part's arrays. A program takes and returns all parts, laid end to end along the dimension named above; an argument that names none is the same for every part. Nothing has to cross between parts.
All inputs are finite; a program needn't handle non-finite values.
Results may differ from the reference program's by a relative error of at most 0.0051.
Values may be sent and summed in bfloat16 or wider, within the bound.
A program may use at most 192 MiB of HBM per device.

```python
import jax
import jax.numpy as jnp

D = 8192
FF = 26624
TOK = 512


def level_of(rng, shape, shards, least, largest):
    loudness, own = 1.0, jax.random.fold_in(rng, 6)
    for axis_at, parts in shards:
        draws = jnp.exp(jax.random.uniform(jax.random.fold_in(own, axis_at), (parts,), jnp.float32, least / len(shards), largest / len(shards)))
        loudness = loudness * jnp.repeat(draws, shape[axis_at] // parts).reshape([-1 if axis == axis_at else 1 for axis in range(len(shape))])
    return loudness


def normal_values(stream_key, shape, deviation, most, shards=(), held_as=jnp.bfloat16):
    gain = level_of(stream_key, shape, shards, -0.22, 0.18) if shards else 1.0
    array = jax.random.normal(stream_key, shape, jnp.float32) * deviation * gain
    return jnp.minimum(jnp.maximum(array, -most), most).astype(held_as)


def setup_inputs(seed: int = 0, part: int = 0) -> dict:
    splits = jax.random.split(jax.random.key(seed), 5)
    own_keys = jax.random.split(jax.random.fold_in(splits[4], part), 5)
    tokens = normal_values(own_keys[0], (TOK, D), 1.0, 6.0, ((0, 4), (1, 4)))
    gate_weight = normal_values(splits[1], (D, FF), D ** -0.5, 0.0625, ((1, 16),))
    up_weight = normal_values(splits[2], (D, FF), D ** -0.5, 0.0625, ((1, 16),))
    down_weight = normal_values(splits[3], (FF, D), FF ** -0.5, 0.0390625, ((0, 4), (1, 4)))
    return dict(tokens=tokens, gate_weight=gate_weight, up_weight=up_weight, down_weight=down_weight)


def reference(tokens, gate_weight, up_weight, down_weight):
    gate_value = jnp.dot(tokens, gate_weight, preferred_element_type=jnp.float32)
    up_value = jnp.dot(tokens, up_weight, preferred_element_type=jnp.float32)
    hidden = (jax.nn.silu(gate_value) * up_value).astype(jnp.bfloat16)
    return jnp.dot(hidden, down_weight, preferred_element_type=jnp.float32).astype(jnp.bfloat16)
```

```python
import jax
import jax.numpy as jnp
from jax import lax
from jax.sharding import PartitionSpec as P

CHUNKS = 2


def shards(tokens, gate_weight, up_weight, down_weight):
    rows = tokens.shape[0] // CHUNKS
    pieces = []
    for at in range(CHUNKS):
        own = tokens[at * rows : (at + 1) * rows]
        wide = lax.all_gather(own, "gx", axis=1, tiled=True)
        pieces.append(lax.all_gather(wide, "gy", axis=0, tiled=True))
    outs = []
    for piece in pieces:
        gate_next = jnp.dot(piece, gate_weight, preferred_element_type=jnp.float32)
        up_next = jnp.dot(piece, up_weight, preferred_element_type=jnp.float32)
        hidden = (jax.nn.silu(gate_next) * up_next).astype(jnp.bfloat16)
        partial_value = jnp.dot(
            lax.all_gather(hidden, "gx", axis=1, tiled=True),
            down_weight,
            preferred_element_type=jnp.float32,
        )
        outs.append(
            lax.psum_scatter(partial_value, "gy", scatter_dimension=0, tiled=True).astype(jnp.bfloat16)
        )
    return jnp.concatenate(outs, axis=0)


def solution(mesh):
    placed = (P(("grp", "gy"), "gx"), P(None, ("gy", "gx")), P(None, ("gy", "gx")), P("gy", "gx"))
    return jax.shard_map(
        shards, mesh=mesh, in_specs=placed, out_specs=P(("grp", "gy"), "gx"), check_vma=False
    )
```

```python
import functools

import jax
import jax.numpy as jnp
from jax import lax
from jax.experimental import pallas as pl
from jax.experimental.pallas import tpu as pltpu
from jax.sharding import PartitionSpec as P

CHUNKS = 2
PARTS = 4
TILE = 128
WIDE = 256


def shards(tokens, gate_weight, up_weight, down_weight):
    rows = tokens.shape[0] // CHUNKS
    pieces = []
    for at in range(CHUNKS):
        own = tokens[at * rows : (at + 1) * rows]
        wide = lax.all_gather(own, "gx", axis=1, tiled=True)
        pieces.append(lax.all_gather(wide, "gy", axis=0, tiled=True))
    outs = []
    for piece in pieces:
        gate_next = jnp.dot(piece, gate_weight, preferred_element_type=jnp.float32)
        up_next = jnp.dot(piece, up_weight, preferred_element_type=jnp.float32)
        hidden = (jax.nn.silu(gate_next) * up_next).astype(jnp.bfloat16)
        partial_value = jnp.dot(
            lax.all_gather(hidden, "gx", axis=1, tiled=True),
            down_weight,
            preferred_element_type=jnp.float32,
        )
        outs.append(
            lax.psum_scatter(partial_value, "gy", scatter_dimension=0, tiled=True).astype(jnp.bfloat16)
        )
    return jnp.concatenate(outs, axis=0)


def kernel(
    nz, tokens, gate, up, down, out,
    tok, hid, wts, dn, acc, r1, r2,
    own_sem, w_sem, dn_sem, tz_s, tz_r, ts_s, ts_r, tx_s, tx_r, tf_s, tf_r, hz_s, hz_r,
    r1_s, r1_r, r2_s, r2_r,
):
    z, g = lax.axis_index("gx"), lax.axis_index("gy")
    core, x = g % 2, g // 2
    sib, across = 2 * x + 1 - core, 2 * (1 - x) + core
    rows = tokens.shape[0] // PARTS
    units = gate.shape[1]
    tiles = units // TILE
    depth = tokens.shape[1]
    f32 = jnp.float32

    def remote(src, dst, s, r, **to):
        return pltpu.make_async_remote_copy(
            src_ref=src, dst_ref=dst, send_sem=s, recv_sem=r, device_id=to,
            device_id_type=pl.DeviceIdType.MESH,
        )

    def token_block(c, who, b):
        place = (who % 2) * 2 + who // 2
        return tok.at[c, b, pl.ds(pl.multiple_of(place * rows, rows), rows), :]

    def hop(view, send, recv, way, c, s):
        b = z - (s - 1) if way == 0 else z + (s - 1)
        to = z + 1 if way == 0 else z - 1
        live = (b >= 0) & (z < nz - 1) if way == 0 else (b < nz) & (z > 0)
        ref = lambda: view(c, b)
        make = lambda: remote(ref(), ref(), send.at[way, c, s - 1], recv.at[way, c, s - 1], gx=to)
        return live, make

    def hop_start(view, send, recv, c, s):
        for way in range(2):
            live, make = hop(view, send, recv, way, c, s)

            @pl.when(live & (s < nz))
            def _():
                make().start()

    def hop_sent(view, send, recv, c, s):
        for way in range(2):
            live, make = hop(view, send, recv, way, c, s)

            @pl.when(live)
            def _():
                make().wait_send()

    def hop_recv(view, send, recv, c, s, then):
        for way in range(2):
            b = z - s if way == 0 else z + s
            back = z - 1 if way == 0 else z + 1

            @pl.when(b >= 0 if way == 0 else b < nz)
            def _():
                remote(
                    view(c, b), view(c, b), send.at[way, c, s - 1], recv.at[way, c, s - 1], gx=back
                ).wait_recv()
                live, make = hop(view, send, recv, way, c, s + 1)

                @pl.when(live)
                def _():
                    make().start()

                if then is not None:
                    then(c, b)

    token_view = lambda c, b: token_block(c, g, b)
    hidden_view = lambda c, b: hid.at[c, b]
    tokens_z = (token_view, tz_s, tz_r)
    hidden_z = (hidden_view, hz_s, hz_r)

    def to_sib(c, b, who, s, r):
        return remote(token_block(c, who, b), token_block(c, who, b), s.at[c, b], r.at[c, b], gy=sib)

    def to_across(c, b, who):
        return remote(
            token_block(c, who, b), token_block(c, who, b), tx_s.at[c, b], tx_r.at[c, b], gy=across
        )

    def spread(c, b):
        to_across(c, b, g).start()
        to_sib(c, b, g, ts_s, ts_r).start()

    def tokens_out(c):
        hop_start(*tokens_z, c, 1)
        spread(c, z)

    def tokens_step(c, s):
        hop_recv(*tokens_z, c, s, spread)

    def tokens_across(c):
        @pl.loop(0, nz)
        def _(b):
            to_across(c, b, across).wait_recv()
            to_sib(c, b, across, tf_s, tf_r).start()

    def tokens_ready(c):
        @pl.loop(0, nz)
        def _(b):
            to_sib(c, b, sib, ts_s, ts_r).wait_recv()
            to_sib(c, b, 2 * (1 - x) + 1 - core, tf_s, tf_r).wait_recv()

    def weight_copies(i):
        t, slot = i % tiles, i % 2
        cols = pl.ds(pl.multiple_of(t * TILE, TILE), TILE)
        return [
            pltpu.make_async_copy(
                ref.at[:, cols], wts.at[slot, :, pl.ds(at * TILE, TILE)], w_sem.at[slot, at]
            )
            for at, ref in enumerate((gate, up))
        ]

    def own_copy(c):
        return pltpu.make_async_copy(
            tokens.at[pl.ds(pl.multiple_of(c * rows, rows), rows), :], token_block(c, g, z), own_sem.at[c]
        )

    for c in range(PARTS):
        own_copy(c).start()
    for copy in weight_copies(0):
        copy.start()
    load_down = pltpu.make_async_copy(down, dn, dn_sem)
    load_down.start()

    barrier = pltpu.get_barrier_semaphore()
    for who in (sib, across):
        pl.semaphore_signal(
            barrier, inc=1, device_id={"gy": who}, device_id_type=pl.DeviceIdType.MESH
        )

    @pl.when(z > 0)
    def _():
        pl.semaphore_signal(
            barrier, inc=1, device_id={"gx": z - 1}, device_id_type=pl.DeviceIdType.MESH
        )

    @pl.when(z < nz - 1)
    def _():
        pl.semaphore_signal(
            barrier, inc=1, device_id={"gx": z + 1}, device_id_type=pl.DeviceIdType.MESH
        )

    pl.semaphore_wait(barrier, 2 + jnp.where(z > 0, 1, 0) + jnp.where(z < nz - 1, 1, 0))

    for c in range(PARTS):
        own_copy(c).wait()
    tokens_out(0)
    tokens_out(1)

    @pl.loop(1, nz)
    def _(s):
        tokens_step(0, s)

    tokens_across(0)

    last = nz - 1
    early = 2 * (PARTS - 1) - 1

    def hidden_step(n):
        hop_recv(*hidden_z, n // last, n % last + 1, None)

    @pl.loop(0, PARTS)
    def _(c):
        tokens_ready(c)

        @pl.loop(0, tiles)
        def _(t):
            i = c * tiles + t

            @pl.when(i + 1 < PARTS * tiles)
            def _():
                for copy in weight_copies(i + 1):
                    copy.start()

            for copy in weight_copies(i):
                copy.wait()
            slot = i % 2
            total = None
            for b in range(nz):
                part = jnp.dot(
                    tok[c, b], wts[slot, pl.ds(b * depth, depth), :], preferred_element_type=f32
                )
                total = part if total is None else total + part
            a, u = total[:, :TILE], total[:, TILE:]
            hid[c, z, :, pl.ds(pl.multiple_of(t * TILE, TILE), TILE)] = (
                a / (1.0 + jnp.exp(-a)) * u
            ).astype(hid.dtype)

            @pl.when((c == 0) & (t < nz * (PARTS - 1)))
            def _():
                which, s = 1 + t // nz, t % nz + 1

                @pl.when((s == 1) & (which + 1 < PARTS))
                def _():
                    tokens_out(which + 1)

                @pl.when(s < nz)
                def _():
                    tokens_step(which, s)

                @pl.when(s == nz)
                def _():
                    tokens_across(which)

            @pl.when((c >= 2) & (t == tiles // 2))
            def _():
                hidden_step(2 * (c - 1) - 1)

        hop_start(*hidden_z, c, 1)

        @pl.when(c >= 1)
        def _():
            hidden_step(2 * (c - 1))

    load_down.wait()

    def mix(d, b, first):
        @pl.loop(0, acc.shape[2] // WIDE)
        def _(n):
            cols = pl.ds(pl.multiple_of(n * WIDE, WIDE), WIDE)
            value = jnp.dot(
                hid[d, b],
                dn[pl.ds(pl.multiple_of(b * units, TILE), units), cols],
                preferred_element_type=f32,
            )
            acc[d, :, cols] = value if first else acc[d, :, cols] + value

    half = 2 * rows
    core_rows = lambda who: pl.ds(pl.multiple_of(who * half, half), half)
    place_rows = lambda at: pl.ds(pl.multiple_of((core * 2 + at) * rows, rows), rows)

    def sum_sib(d):
        return remote(acc.at[d, core_rows(1 - core)], r1.at[d], r1_s.at[d], r1_r.at[d], gy=sib)

    def sum_across(d):
        return remote(acc.at[d, place_rows(1 - x)], r2.at[d], r2_s.at[d], r2_r.at[d], gy=across)

    def second(d):
        sum_sib(d).wait_recv()
        acc[d, core_rows(core), :] += r1[d]
        sum_across(d).start()

    def third(d):
        sum_across(d).wait_recv()
        out[pl.ds(pl.multiple_of(d * rows, rows), rows), :] = (
            acc[d, place_rows(x), :] + r2[d]
        ).astype(out.dtype)

    @pl.loop(0, PARTS)
    def _(d):
        mix(d, z, True)

        @pl.loop(1, nz)
        def _(s):
            n = d * last + s - 1

            @pl.when(n >= early)
            def _():
                hidden_step(n)

            @pl.when(z - s >= 0)
            def _():
                mix(d, z - s, False)

            @pl.when(z + s < nz)
            def _():
                mix(d, z + s, False)

        sum_sib(d).start()

        @pl.when(d >= 1)
        def _():
            second(d - 1)

        @pl.when(d >= 2)
        def _():
            third(d - 2)

    second(PARTS - 1)
    third(PARTS - 2)
    third(PARTS - 1)

    @pl.loop(0, PARTS)
    def _(c):
        @pl.loop(1, nz)
        def _(s):
            hop_sent(*tokens_z, c, s)
            hop_sent(*hidden_z, c, s)

        @pl.loop(0, nz)
        def _(b):
            to_across(c, b, g).wait_send()
            to_sib(c, b, g, ts_s, ts_r).wait_send()
            to_sib(c, b, across, tf_s, tf_r).wait_send()

        sum_sib(c).wait_send()
        sum_across(c).wait_send()


def fused(nz, tokens, gate_weight, up_weight, down_weight):
    own, depth = tokens.shape
    units, cols = gate_weight.shape[1], down_weight.shape[1]
    rows = own // PARTS
    whole = 4 * rows
    dma = pltpu.SemaphoreType.DMA
    bf16 = jnp.bfloat16
    anywhere = pl.BlockSpec(memory_space=pl.ANY)
    hops, each = dma((2, PARTS, nz - 1)), dma((PARTS, nz))
    one = dma((PARTS,))
    return pl.pallas_call(
        functools.partial(kernel, nz),
        out_shape=jax.ShapeDtypeStruct((own, cols), bf16),
        in_specs=[anywhere] * 4,
        out_specs=pl.BlockSpec(memory_space=pltpu.VMEM),
        scratch_shapes=[
            pltpu.VMEM((PARTS, nz, whole, depth), bf16),
            pltpu.VMEM((PARTS, nz, whole, units), bf16),
            pltpu.VMEM((2, nz * depth, 2 * TILE), bf16),
            pltpu.VMEM(down_weight.shape, bf16),
            pltpu.VMEM((PARTS, whole, cols), jnp.float32),
            pltpu.VMEM((PARTS, 2 * rows, cols), jnp.float32),
            pltpu.VMEM((PARTS, rows, cols), jnp.float32),
            one, dma((2, 2)), dma(()),
            hops, hops, each, each, each, each, each, each, hops, hops,
            one, one, one, one,
        ],
        compiler_params=pltpu.CompilerParams(
            collective_id=0, has_side_effects=True, vmem_limit_bytes=62 * 2**20
        ),
        cost_estimate=pl.CostEstimate(
            flops=2 * 4 * own * (2 * nz * depth * units + nz * units * cols),
            bytes_accessed=2 * (2 * PARTS * nz * depth * units + nz * units * cols),
            transcendentals=4 * own * units,
        ),
    )(tokens, gate_weight, up_weight, down_weight)


def fits(mesh):
    def body(nz, tokens, gate_weight, up_weight, down_weight):
        own, depth = tokens.shape
        units, cols = gate_weight.shape[1], down_weight.shape[1]
        held = (
            2 * 4 * own * nz * (depth + units) + 8 * nz * depth * TILE
            + 2 * nz * units * cols + 4 * own * cols * 7 + 2 * own * cols
        )
        tiles = units // TILE
        return (
            mesh.shape["gy"] == 4 and nz > 1 and own % (16 * PARTS) == 0 and units % TILE == 0
            and depth % TILE == 0 and cols % WIDE == 0 and held <= 61 * 2**20
            and tiles >= nz * (PARTS - 1) and (PARTS - 1) * 2 - 1 <= PARTS * (nz - 1)
        )
    return body


def solution(mesh):
    placed = (P(("grp", "gy"), "gx"), P(None, ("gy", "gx")), P(None, ("gy", "gx")), P("gy", "gx"))
    nz = mesh.shape["gx"]
    ok = fits(mesh)

    def body(*args):
        return fused(nz, *args) if ok(nz, *args) else shards(*args)

    return jax.shard_map(
        body, mesh=mesh, in_specs=placed, out_specs=P(("grp", "gy"), "gx"), check_vma=False
    )
```

```python
import functools

import jax
import jax.numpy as jnp
from jax import lax
from jax.experimental import pallas as pl
from jax.experimental.pallas import tpu as pltpu
from jax.sharding import PartitionSpec as P

CHUNKS = 2
PARTS = 2
TILE = 128
WIDE = 256


def shards(tokens, gate_weight, up_weight, down_weight):
    rows = tokens.shape[0] // CHUNKS
    pieces = []
    for at in range(CHUNKS):
        own = tokens[at * rows : (at + 1) * rows]
        wide = lax.all_gather(own, "gx", axis=1, tiled=True)
        pieces.append(lax.all_gather(wide, "gy", axis=0, tiled=True))
    outs = []
    for piece in pieces:
        gate_next = jnp.dot(piece, gate_weight, preferred_element_type=jnp.float32)
        up_next = jnp.dot(piece, up_weight, preferred_element_type=jnp.float32)
        hidden = (jax.nn.silu(gate_next) * up_next).astype(jnp.bfloat16)
        partial_value = jnp.dot(
            lax.all_gather(hidden, "gx", axis=1, tiled=True),
            down_weight,
            preferred_element_type=jnp.float32,
        )
        outs.append(
            lax.psum_scatter(partial_value, "gy", scatter_dimension=0, tiled=True).astype(jnp.bfloat16)
        )
    return jnp.concatenate(outs, axis=0)


def kernel(
    nz, tokens, gate, up, down, out,
    tok, hid, wts, dn, acc, r1, r2,
    own_sem, w_sem, dn_sem, tz_s, tz_r, ts_s, ts_r, tx_s, tx_r, tf_s, tf_r, hz_s, hz_r,
    r1_s, r1_r, r2_s, r2_r,
):
    z, g = lax.axis_index("gx"), lax.axis_index("gy")
    core, x = g % 2, g // 2
    sib, across = 2 * x + 1 - core, 2 * (1 - x) + core
    rows = tokens.shape[0] // PARTS
    units = gate.shape[1]
    tiles = units // TILE
    depth = tokens.shape[1]
    f32 = jnp.float32

    def remote(src, dst, s, r, **to):
        return pltpu.make_async_remote_copy(
            src_ref=src, dst_ref=dst, send_sem=s, recv_sem=r, device_id=to,
            device_id_type=pl.DeviceIdType.MESH,
        )

    def token_block(c, who, b):
        place = (who % 2) * 2 + who // 2
        return tok.at[c, b, pl.ds(pl.multiple_of(place * rows, rows), rows), :]

    def hop(view, send, recv, way, c, s):
        b = z - (s - 1) if way == 0 else z + (s - 1)
        to = z + 1 if way == 0 else z - 1
        live = (b >= 0) & (z < nz - 1) if way == 0 else (b < nz) & (z > 0)
        ref = lambda: view(c, b)
        make = lambda: remote(ref(), ref(), send.at[way, c, s - 1], recv.at[way, c, s - 1], gx=to)
        return live, make

    def hop_start(view, send, recv, c, s):
        for way in range(2):
            live, make = hop(view, send, recv, way, c, s)

            @pl.when(live & (s < nz))
            def _():
                make().start()

    def hop_sent(view, send, recv, c, s):
        for way in range(2):
            live, make = hop(view, send, recv, way, c, s)

            @pl.when(live)
            def _():
                make().wait_send()

    def hop_recv(view, send, recv, c, s, then):
        for way in range(2):
            b = z - s if way == 0 else z + s
            back = z - 1 if way == 0 else z + 1

            @pl.when(b >= 0 if way == 0 else b < nz)
            def _():
                remote(
                    view(c, b), view(c, b), send.at[way, c, s - 1], recv.at[way, c, s - 1], gx=back
                ).wait_recv()
                live, make = hop(view, send, recv, way, c, s + 1)

                @pl.when(live)
                def _():
                    make().start()

                if then is not None:
                    then(c, b)

    token_view = lambda c, b: token_block(c, g, b)
    cut = (tiles + 1) // 2
    spans = ((0, cut * TILE), (cut * TILE, units - cut * TILE))
    pieces_z = [
        (lambda p, b, span=span: hid.at[p // 2, b, :, pl.ds(*span)], hz_s, hz_r) for span in spans
    ]
    tokens_z = (token_view, tz_s, tz_r)

    def to_sib(c, b, who, s, r):
        return remote(token_block(c, who, b), token_block(c, who, b), s.at[c, b], r.at[c, b], gy=sib)

    def to_across(c, b, who):
        return remote(
            token_block(c, who, b), token_block(c, who, b), tx_s.at[c, b], tx_r.at[c, b], gy=across
        )

    def spread(c, b):
        to_across(c, b, g).start()
        to_sib(c, b, g, ts_s, ts_r).start()

    def tokens_out(c):
        hop_start(*tokens_z, c, 1)
        spread(c, z)

    def tokens_step(c, s):
        hop_recv(*tokens_z, c, s, spread)

    def tokens_across(c):
        @pl.loop(0, nz)
        def _(b):
            to_across(c, b, across).wait_recv()
            to_sib(c, b, across, tf_s, tf_r).start()

    def tokens_ready(c):
        @pl.loop(0, nz)
        def _(b):
            to_sib(c, b, sib, ts_s, ts_r).wait_recv()
            to_sib(c, b, 2 * (1 - x) + 1 - core, tf_s, tf_r).wait_recv()

    def weight_copies(i):
        t, slot = i % tiles, i % 2
        cols = pl.ds(pl.multiple_of(t * TILE, TILE), TILE)
        return [
            pltpu.make_async_copy(
                ref.at[:, cols], wts.at[slot, :, pl.ds(at * TILE, TILE)], w_sem.at[slot, at]
            )
            for at, ref in enumerate((gate, up))
        ]

    def own_copy(c):
        return pltpu.make_async_copy(
            tokens.at[pl.ds(pl.multiple_of(c * rows, rows), rows), :], token_block(c, g, z), own_sem.at[c]
        )

    for c in range(PARTS):
        own_copy(c).start()
    for copy in weight_copies(0):
        copy.start()
    load_down = pltpu.make_async_copy(down, dn, dn_sem)
    load_down.start()

    barrier = pltpu.get_barrier_semaphore()
    for who in (sib, across):
        pl.semaphore_signal(
            barrier, inc=1, device_id={"gy": who}, device_id_type=pl.DeviceIdType.MESH
        )

    @pl.when(z > 0)
    def _():
        pl.semaphore_signal(
            barrier, inc=1, device_id={"gx": z - 1}, device_id_type=pl.DeviceIdType.MESH
        )

    @pl.when(z < nz - 1)
    def _():
        pl.semaphore_signal(
            barrier, inc=1, device_id={"gx": z + 1}, device_id_type=pl.DeviceIdType.MESH
        )

    pl.semaphore_wait(barrier, 2 + jnp.where(z > 0, 1, 0) + jnp.where(z < nz - 1, 1, 0))

    for c in range(PARTS):
        own_copy(c).wait()
    tokens_out(0)
    tokens_out(1)

    @pl.loop(1, nz)
    def _(s):
        tokens_step(0, s)

    tokens_across(0)

    last = nz - 1
    events = nz * (PARTS - 1)
    stride = (tiles - 1) // events

    def hidden_step(n):
        p = n // last
        for side in range(2):

            @pl.when(p % 2 == side)
            def _():
                hop_recv(*pieces_z[side], p, n % last + 1, None)

    @pl.loop(0, PARTS)
    def _(c):
        tokens_ready(c)

        @pl.loop(0, tiles)
        def _(t):
            i = c * tiles + t

            @pl.when(i + 1 < PARTS * tiles)
            def _():
                for copy in weight_copies(i + 1):
                    copy.start()

            for copy in weight_copies(i):
                copy.wait()
            slot = i % 2
            total = None
            for b in range(nz):
                part = jnp.dot(
                    tok[c, b], wts[slot, pl.ds(b * depth, depth), :], preferred_element_type=f32
                )
                total = part if total is None else total + part
            a, u = total[:, :TILE], total[:, TILE:]
            hid[c, z, :, pl.ds(pl.multiple_of(t * TILE, TILE), TILE)] = (
                a / (1.0 + jnp.exp(-a)) * u
            ).astype(hid.dtype)

            @pl.when((c == 0) & (t % stride == 0) & (t >= stride) & (t <= stride * events))
            def _():
                q = t // stride - 1
                which, s = 1 + q // nz, q % nz + 1

                @pl.when((s == 1) & (which + 1 < PARTS))
                def _():
                    tokens_out(which + 1)

                @pl.when(s < nz)
                def _():
                    tokens_step(which, s)

                @pl.when(s == nz)
                def _():
                    tokens_across(which)

            for side, (done, middle) in enumerate(((cut - 1, cut // 2), (tiles - 1, cut + 2))):
                p = 2 * c + side

                @pl.when((t == middle) & (p >= 2))
                def _():
                    hidden_step(2 * (p - 1) - 1)

                @pl.when(t == done)
                def _():
                    hop_start(*pieces_z[side], p, 1)

                    @pl.when(p >= 1)
                    def _():
                        hidden_step(2 * (p - 1))

    load_down.wait()

    def mix(d, b, first):
        @pl.loop(0, acc.shape[2] // WIDE)
        def _(n):
            cols = pl.ds(pl.multiple_of(n * WIDE, WIDE), WIDE)
            value = jnp.dot(
                hid[d, b],
                dn[pl.ds(pl.multiple_of(b * units, TILE), units), cols],
                preferred_element_type=f32,
            )
            acc[d, :, cols] = value if first else acc[d, :, cols] + value

    half = 2 * rows
    core_rows = lambda who: pl.ds(pl.multiple_of(who * half, half), half)
    place_rows = lambda at: pl.ds(pl.multiple_of((core * 2 + at) * rows, rows), rows)

    def sum_sib(d):
        return remote(acc.at[d, core_rows(1 - core)], r1.at[d], r1_s.at[d], r1_r.at[d], gy=sib)

    def sum_across(d):
        return remote(acc.at[d, place_rows(1 - x)], r2.at[d], r2_s.at[d], r2_r.at[d], gy=across)

    def second(d):
        sum_sib(d).wait_recv()
        acc[d, core_rows(core), :] += r1[d]
        sum_across(d).start()

    def third(d):
        sum_across(d).wait_recv()
        out[pl.ds(pl.multiple_of(d * rows, rows), rows), :] = (
            acc[d, place_rows(x), :] + r2[d]
        ).astype(out.dtype)

    @pl.loop(0, PARTS)
    def _(d):
        mix(d, z, True)

        @pl.when(d >= 1)
        def _():
            hidden_step(7)

        @pl.loop(1, nz)
        def _(s):
            m = d * nz + s

            @pl.when((m >= 2) & (m <= 5))
            def _():
                hidden_step(m + 3)

            @pl.when(m >= 5)
            def _():
                hidden_step(m + 4)

            @pl.when(z - s >= 0)
            def _():
                mix(d, z - s, False)

            @pl.when(z + s < nz)
            def _():
                mix(d, z + s, False)

        sum_sib(d).start()

        @pl.when(d >= 1)
        def _():
            second(d - 1)

        @pl.when(d >= 2)
        def _():
            third(d - 2)

    second(PARTS - 1)
    third(PARTS - 2)
    third(PARTS - 1)

    @pl.loop(0, PARTS)
    def _(c):
        @pl.loop(1, nz)
        def _(s):
            hop_sent(*tokens_z, c, s)
            for side in range(2):
                hop_sent(*pieces_z[side], 2 * c + side, s)

        @pl.loop(0, nz)
        def _(b):
            to_across(c, b, g).wait_send()
            to_sib(c, b, g, ts_s, ts_r).wait_send()
            to_sib(c, b, across, tf_s, tf_r).wait_send()

        sum_sib(c).wait_send()
        sum_across(c).wait_send()


def fused(nz, tokens, gate_weight, up_weight, down_weight):
    own, depth = tokens.shape
    units, cols = gate_weight.shape[1], down_weight.shape[1]
    rows = own // PARTS
    whole = 4 * rows
    dma = pltpu.SemaphoreType.DMA
    bf16 = jnp.bfloat16
    anywhere = pl.BlockSpec(memory_space=pl.ANY)
    hops, each = dma((2, PARTS, nz - 1)), dma((PARTS, nz))
    one, pieces = dma((PARTS,)), dma((2, 2 * PARTS, nz - 1))
    return pl.pallas_call(
        functools.partial(kernel, nz),
        out_shape=jax.ShapeDtypeStruct((own, cols), bf16),
        in_specs=[anywhere] * 4,
        out_specs=pl.BlockSpec(memory_space=pltpu.VMEM),
        scratch_shapes=[
            pltpu.VMEM((PARTS, nz, whole, depth), bf16),
            pltpu.VMEM((PARTS, nz, whole, units), bf16),
            pltpu.VMEM((2, nz * depth, 2 * TILE), bf16),
            pltpu.VMEM(down_weight.shape, bf16),
            pltpu.VMEM((PARTS, whole, cols), jnp.float32),
            pltpu.VMEM((PARTS, 2 * rows, cols), jnp.float32),
            pltpu.VMEM((PARTS, rows, cols), jnp.float32),
            one, dma((2, 2)), dma(()),
            hops, hops, each, each, each, each, each, each, pieces, pieces,
            one, one, one, one,
        ],
        compiler_params=pltpu.CompilerParams(
            collective_id=0, has_side_effects=True, vmem_limit_bytes=62 * 2**20
        ),
        cost_estimate=pl.CostEstimate(
            flops=2 * 4 * own * (2 * nz * depth * units + nz * units * cols),
            bytes_accessed=2 * (2 * PARTS * nz * depth * units + nz * units * cols),
            transcendentals=4 * own * units,
        ),
    )(tokens, gate_weight, up_weight, down_weight)


def fits(mesh):
    def body(nz, tokens, gate_weight, up_weight, down_weight):
        own, depth = tokens.shape
        units, cols = gate_weight.shape[1], down_weight.shape[1]
        held = (
            2 * 4 * own * nz * (depth + units) + 8 * nz * depth * TILE
            + 2 * nz * units * cols + 4 * own * cols * 7 + 2 * own * cols
        )
        tiles = units // TILE
        return (
            mesh.shape["gy"] == 4 and nz == 4 and own % (16 * PARTS) == 0 and units % TILE == 0
            and depth % TILE == 0 and cols % WIDE == 0 and held <= 61 * 2**20
            and tiles > nz * (PARTS - 1) and tiles >= 9
        )
    return body


def solution(mesh):
    placed = (P(("grp", "gy"), "gx"), P(None, ("gy", "gx")), P(None, ("gy", "gx")), P("gy", "gx"))
    nz = mesh.shape["gx"]
    ok = fits(mesh)

    def body(*args):
        return fused(nz, *args) if ok(nz, *args) else shards(*args)

    return jax.shard_map(
        body, mesh=mesh, in_specs=placed, out_specs=P(("grp", "gy"), "gx"), check_vma=False
    )
```
